32 devices in a mesh: ctx: 8 (over z, y), tp: 4 (over x, core).
Axes of the slice: x: 2, y: 2, z: 4, core: 2. Of those that a mesh axis runs over, the one named last changes fastest.
Arguments:
- features: bfloat16 [1024, 3, 4096], P('ctx', None, 'tp'), may hold values from -6 to 6
- short_taps: float32 [3, 3, 4096], P(None, None, 'tp'), may hold values from -3 to 3
- residues: float32 [16, 4096], P(None, 'tp'), may hold values from -2 to 2
- log_rate: float32 [16, 4096], P(None, 'tp'), may hold values from -13 to -3.5, as said below
- out_weight: bfloat16 [4096, 8192], P('tp'), may hold values from -0.09375 to 0.09375
- grad_out: bfloat16 [1024, 8192], P('ctx', 'tp'), may hold values from -6 to 6
Outputs:
- grad_features: bfloat16 [1024, 3, 4096], P('ctx', None, 'tp')
- grad_taps: float32 [3, 3, 4096], P(None, None, 'tp')
- grad_residues: float32 [16, 4096], P(None, 'tp')
- grad_log_rate: float32 [16, 4096], P(None, 'tp')
- grad_weight_t: float32 [8192, 4096], P('ctx', 'tp')
The draws below stay inside these ranges and needn't reach their ends.
Inputs may be any that keep to these rules, and one draw needn't show every extreme that they name: `log_rate`: log of a decay rate per token.
All inputs are finite; a program needn't handle non-finite values.
Results may differ from the reference program's by a relative error of at most 0.0058.
Values may be sent and summed in bfloat16 or wider, within the bound.
A program may use at most 192 MiB of HBM per device.

```python
import jax
import jax.numpy as jnp
from jax import lax

D = 8192
C = 4096
R = 16
KS = 3
TOKENS = 1024


def draw_log_rate(key, part):
    uniform_draw = jax.random.uniform(key, (R, C), jnp.float32)
    lowest = jnp.log(0.1 / TOKENS)
    fastest = jnp.log(0.03)
    return lowest + uniform_draw * (fastest - lowest)


def raised(result, stream_key, source, target, blocks, factor):
    owner, partner = [(jnp.arange(result.shape[axis_at]) // (result.shape[axis_at] // blocks)).reshape([-1 if axis == axis_at else 1 for axis in range(result.ndim)]) for axis_at in (source, target)]
    chosen = jax.random.permutation(stream_key, blocks)[partner]
    strong = (owner == chosen) | (owner == (partner + blocks // 2) % blocks)
    return jnp.where(strong, factor * result, result)


def steps_of(stream_key, extent, split, least, high):
    level = 1.0
    for position, parts in split:
        draws = jax.random.uniform(jax.random.fold_in(jax.random.fold_in(stream_key, 6), position), (parts,), jnp.float32, least / len(split), high / len(split))
        level = level * jnp.repeat(jnp.exp(draws), extent[position] // parts).reshape((-1,) + (1,) * (len(extent) - 1 - position))
    return level


def scatter_about(own_key, extent, width, reach, cuts=(), kind=jnp.bfloat16):
    level = steps_of(own_key, extent, cuts, -0.22, 0.18) if cuts else 1.0
    entries = jax.random.normal(own_key, extent, jnp.float32) * width * level
    return jnp.minimum(jnp.maximum(entries, -reach), reach).astype(kind)


def gaussian_with(stream_key, extent, spread, reach, cuts, heavy, dtype=jnp.bfloat16):
    drawn = spread * jax.random.normal(stream_key, extent, jnp.float32)
    if cuts:
        drawn = drawn * steps_of(stream_key, extent, cuts, -0.22, 0.18)
    return jnp.clip(raised(drawn, jax.random.fold_in(stream_key, 3), *heavy), -reach, reach).astype(dtype)


def setup_inputs(seed: int = 0) -> dict:
    streams_of = jax.random.split(jax.random.key(seed), 7)
    features = scatter_about(streams_of[0], (TOKENS, 3, C), 1.0, 6.0, ((0, 8), (2, 4)))
    short_taps = scatter_about(streams_of[1], (KS, 3, C), 0.6, 3.0, ((2, 4),), jnp.float32)
    residues = scatter_about(streams_of[2], (R, C), 0.35, 2.0, ((1, 4),), jnp.float32)
    log_rate = draw_log_rate(jax.random.fold_in(streams_of[6], 71), 0)
    out_weight = scatter_about(streams_of[4], (C, D), C ** -0.5, 0.09375, ((0, 4),))
    grad_out = gaussian_with(streams_of[5], (TOKENS, D), 1.0, 6.0, ((0, 8), (1, 4)), (0, 1, 8, 2.0))
    return dict(features=features, short_taps=short_taps, residues=residues, log_rate=log_rate, out_weight=out_weight, grad_out=grad_out)


def long_conv(product, residues, log_rate):
    block_len = 128
    length, channels = product.shape
    block_count = length // block_len
    decay_rate = jnp.exp(log_rate)
    amplitude = residues * jnp.exp(0.5 * log_rate)
    lag_steps = jnp.arange(block_len).astype(jnp.float32)
    kernel = lax.optimization_barrier(jnp.sum(amplitude[:, None, :] * jnp.exp(-decay_rate[:, None, :] * lag_steps[None, :, None]), axis=0))
    row_ids = jnp.arange(block_len)[:, None]
    col_ids = jnp.arange(block_len)[None, :]
    distance = row_ids - col_ids
    toeplitz = jnp.where((distance >= 0)[:, :, None], kernel[jnp.maximum(distance, 0)], 0.0)
    blocks = product.reshape(block_count, block_len, channels)
    inside = jnp.einsum('ijc,bjc->bic', toeplitz, blocks, precision=lax.Precision.HIGHEST)
    injection = jnp.exp(-decay_rate[:, None, :] * (block_len - 1 - lag_steps)[None, :, None])
    entering = jnp.einsum('rjc,bjc->brc', injection, blocks, precision=lax.Precision.HIGHEST)
    carry_decay = jnp.broadcast_to(jnp.exp(-decay_rate * block_len), entering.shape)

    def combine(first, second):
        return (first[0] * second[0], second[0] * first[1] + second[1])
    unused, states = lax.associative_scan(combine, (carry_decay, entering), axis=0)
    before = jnp.concatenate([jnp.zeros_like(states[:1]), states[:-1]], axis=0)
    readout = amplitude[:, None, :] * jnp.exp(-decay_rate[:, None, :] * (lag_steps + 1.0)[None, :, None])
    from_past = jnp.einsum('ric,brc->bic', readout, before, precision=lax.Precision.HIGHEST)
    return (inside + from_past).reshape(length, channels)

def reference(features, short_taps, residues, log_rate, out_weight, grad_out):
    length = features.shape[0]
    tap_count = short_taps.shape[0]
    padded_in = jnp.pad(features.astype(jnp.float32), ((tap_count - 1, 0), (0, 0), (0, 0)))
    shortened = sum((short_taps[lag] * padded_in[tap_count - 1 - lag:tap_count - 1 - lag + length] for lag in range(tap_count)))
    product = (shortened[:, 1] * shortened[:, 2]).astype(jnp.bfloat16)
    product_f = lax.optimization_barrier(product).astype(jnp.float32)
    conv_f, pullback = jax.vjp(long_conv, product_f, residues, log_rate)
    convolved = lax.optimization_barrier(conv_f.astype(jnp.bfloat16)).astype(jnp.float32)
    gated = (shortened[:, 0] * convolved).astype(jnp.bfloat16)
    grad_weight_t = lax.dot_general(grad_out, gated, (((0,), (0,)), ((), ())), preferred_element_type=jnp.float32)
    grad_gated = lax.dot_general(grad_out, out_weight, (((1,), (1,)), ((), ())), preferred_element_type=jnp.float32)
    grad_conv = lax.optimization_barrier((grad_gated * shortened[:, 0]).astype(jnp.bfloat16)).astype(jnp.float32)
    grad_prod_f, grad_residues, grad_log_rate = pullback(grad_conv)
    grad_product = lax.optimization_barrier(grad_prod_f.astype(jnp.bfloat16)).astype(jnp.float32)
    grad_short = jnp.stack([grad_gated * convolved, grad_product * shortened[:, 2], grad_product * shortened[:, 1]], axis=1)
    grad_taps = jnp.stack([lax.optimization_barrier(jnp.sum(grad_short * padded_in[tap_count - 1 - lag:tap_count - 1 - lag + length], axis=0)) for lag in range(tap_count)], axis=0)
    tail_pad = jnp.pad(grad_short, ((0, tap_count - 1), (0, 0), (0, 0)))
    grad_features = sum((short_taps[lag] * tail_pad[lag:lag + length] for lag in range(tap_count)))
    return (grad_features.astype(jnp.bfloat16), grad_taps, grad_residues, grad_log_rate, grad_weight_t)
```

```python
import functools

import jax
import jax.numpy as jnp
from jax import lax
from jax.experimental import pallas as pl
from jax.experimental.pallas import tpu as pltpu
from jax.sharding import PartitionSpec as P

F32 = jnp.float32
BF16 = jnp.bfloat16
LANES = 128


def shifted(value, axis, steps):
    count = lax.axis_size(axis)
    first, last = (max(0, -steps), min(count, count - steps))
    return lax.ppermute(value, axis, [(source, source + steps) for source in range(first, last)])


def rounded(value):
    return value.astype(BF16).astype(F32)


def local_states_forward(padded_ref, taps_ref, decay_ref, short_ref, state_ref):
    modes = decay_ref.shape[0]
    length = short_ref.shape[0]
    tap_count = taps_ref.shape[0]

    def filter_step(t, carry):
        for j in range(3):
            total = taps_ref[0, j] * padded_ref[t + tap_count - 1, j]
            for lag in range(1, tap_count):
                total = total + taps_ref[lag, j] * padded_ref[t + tap_count - 1 - lag, j]
            short_ref[t, j] = total
        return carry

    lax.fori_loop(0, length, filter_step, 0, unroll=4)
    decays = [decay_ref[r] for r in range(modes)]

    def step(t, states):
        product = rounded(short_ref[t, 1] * short_ref[t, 2])
        return tuple(decays[r] * states[r] + product for r in range(modes))

    zero = jnp.zeros(decay_ref.shape[1:], F32)
    final = lax.fori_loop(0, length, step, (zero,) * modes, unroll=4)
    for r in range(modes):
        state_ref[r] = final[r]


def local_states_backward(grad_conv_ref, decay_ref, state_ref):
    modes = decay_ref.shape[0]
    length = grad_conv_ref.shape[0]
    decays = [decay_ref[r] for r in range(modes)]

    def step(i, states):
        grad = grad_conv_ref[length - 1 - i]
        return tuple(decays[r] * states[r] + grad for r in range(modes))

    zero = jnp.zeros(decay_ref.shape[1:], F32)
    final = lax.fori_loop(0, length, step, (zero,) * modes, unroll=4)
    for r in range(modes):
        state_ref[r] = final[r]


def full_scans(
    padded_ref, short_ref, grad_gated_ref, grad_conv_ref, decay_ref, amp_ref, past_ref, future_ref,
    gated_ref, grad_short_ref, taps_out_ref, grad_amp_ref, grad_decay_ref,
    history, readout,
):
    modes = decay_ref.shape[0]
    length = short_ref.shape[0]
    tap_count = taps_out_ref.shape[0]
    zero = jnp.zeros(decay_ref.shape[1:], F32)
    decays = [decay_ref[r] for r in range(modes)]
    amps = [amp_ref[r] for r in range(modes)]
    for r in range(modes):
        history[0, r] = past_ref[r]

    def forward(t, states):
        product = rounded(short_ref[t, 1] * short_ref[t, 2])
        new = tuple(decays[r] * states[r] + product for r in range(modes))
        terms = [amps[r] * new[r] for r in range(modes)]
        for r in range(modes):
            history[t + 1, r] = new[r]
        while len(terms) > 1:
            terms = [terms[i] + terms[i + 1] for i in range(0, len(terms), 2)]
        convolved = rounded(terms[0])
        gated_ref[t] = short_ref[t, 0] * convolved
        grad_short_ref[t, 0] = grad_gated_ref[t] * convolved
        return new

    lax.fori_loop(0, length, forward, tuple(past_ref[r] for r in range(modes)), unroll=2)

    half = modes // 2
    for group in range(2):
        picks = list(range(group * half, group * half + half))

        def backward(i, carry):
            t = length - 1 - i
            states, grad_amp, grad_decay = carry
            grad = grad_conv_ref[t]
            new = tuple(decays[r] * states[k] + grad for k, r in enumerate(picks))
            terms = [amps[r] * new[k] for k, r in enumerate(picks)]
            grad_amp = tuple(grad_amp[k] + grad * history[t + 1, r] for k, r in enumerate(picks))
            grad_decay = tuple(grad_decay[k] + new[k] * history[t, r] for k, r in enumerate(picks))
            while len(terms) > 1:
                terms = [terms[i] + terms[i + 1] for i in range(0, len(terms), 2)]
            if group == 0:
                readout[t] = terms[0]
            else:
                grad_product = rounded(readout[t] + terms[0])
                grad_short_ref[t, 1] = grad_product * short_ref[t, 2]
                grad_short_ref[t, 2] = grad_product * short_ref[t, 1]
            return new, grad_amp, grad_decay

        start = (tuple(future_ref[r] for r in picks), (zero,) * half, (zero,) * half)
        unused, grad_amp, grad_decay = lax.fori_loop(0, length, backward, start, unroll=2)
        for k, r in enumerate(picks):
            grad_amp_ref[r] = grad_amp[k]
            grad_decay_ref[r] = grad_decay[k]

    def taps_step(t, sums):
        new = []
        for j in range(3):
            grad = grad_short_ref[t, j]
            for lag in range(tap_count):
                new.append(sums[j * tap_count + lag] + grad * padded_ref[t + tap_count - 1 - lag, j])
        return tuple(new)

    sums = lax.fori_loop(0, length, taps_step, (zero,) * (3 * tap_count), unroll=4)
    for j in range(3):
        for lag in range(tap_count):
            taps_out_ref[lag, j] = sums[j * tap_count + lag]


def call(kernel, outs, scratch=(), mib=48):
    return pl.pallas_call(
        kernel,
        out_shape=[jax.ShapeDtypeStruct(shape, F32) for shape in outs],
        scratch_shapes=[pltpu.VMEM(shape, F32) for shape in scratch],
        compiler_params=pltpu.CompilerParams(vmem_limit_bytes=mib * 2**20),
    )


def per_device(features, short_taps, residues, log_rate, out_weight, grad_out):
    length, triple, width = features.shape
    tap_count = short_taps.shape[0]
    modes = residues.shape[0]
    groups = lax.axis_size("ctx")
    ranks = lax.axis_size("tp")
    position = lax.axis_index("ctx")
    rank = lax.axis_index("tp")
    rows = width // LANES
    tile = (rows, LANES)

    cotangent = lax.all_gather(grad_out, "tp", axis=1, tiled=True)
    rim_rows = shifted(features[length - (tap_count - 1) :], "ctx", 1)
    padded = jnp.concatenate([rim_rows, features], axis=0).astype(F32)
    padded = padded.reshape((length + tap_count - 1, triple) + tile)
    taps = short_taps.reshape((tap_count, triple) + tile)
    half_rate = jnp.exp(0.5 * log_rate).reshape((modes,) + tile)
    rate = jnp.exp(log_rate).reshape((modes,) + tile)
    amp = residues.reshape((modes,) + tile) * half_rate
    decay = jnp.exp(-rate)
    block_decay = jnp.exp(-rate * length)

    short, past_local = call(
        local_states_forward, [(length, triple) + tile, (modes,) + tile]
    )(padded, taps, decay)

    grad_gated = lax.dot_general(
        cotangent, out_weight, (((1,), (1,)), ((), ())), preferred_element_type=F32
    ).reshape((length,) + tile)
    grad_conv = rounded(grad_gated * short[:, 0])
    (future_local,) = call(local_states_backward, [(modes,) + tile])(grad_conv, decay)

    states = lax.all_gather(jnp.stack([past_local, future_local]), "ctx", axis=0)
    past = jnp.zeros((modes,) + tile, F32)
    future = past
    for block in range(groups - 1):
        past = jnp.where(block < position, block_decay * past + states[block, 0], past)
    for block in range(groups - 1, 0, -1):
        future = jnp.where(block > position, block_decay * future + states[block, 1], future)

    features_out = cotangent.shape[1]
    share = features_out // (groups * ranks)
    mine = lax.dynamic_index_in_dim(
        cotangent.reshape(length, groups, ranks, share), rank, 2, keepdims=False
    )
    swapped = lax.all_to_all(
        mine.reshape(length, groups * share), "ctx", split_axis=1, concat_axis=0, tiled=True
    )
    block_cotangent = lax.all_gather(swapped, "tp", axis=1, tiled=True)

    gated, grad_short, part_taps, grad_amp, grad_decay = call(
        full_scans,
        [(length,) + tile, (length, triple) + tile, (tap_count, triple) + tile]
        + [(modes,) + tile] * 2,
        [(length + 1, modes) + tile, (length,) + tile],
    )(padded, short, grad_gated, grad_conv, decay, amp, past, future)

    gated_all = lax.all_gather(
        gated.astype(BF16).reshape(length, width), "ctx", axis=0, tiled=True
    )
    grad_weight_t = lax.dot_general(
        block_cotangent, gated_all, (((0,), (0,)), ((), ())), preferred_element_type=F32
    )

    tail_rows = shifted(grad_short[: tap_count - 1], "ctx", -1)
    tail_pad = jnp.concatenate([grad_short, tail_rows], axis=0)
    grad_features = sum(taps[lag] * tail_pad[lag : lag + length] for lag in range(tap_count))
    packed = jnp.concatenate(
        [part_taps.reshape((tap_count * triple,) + tile), grad_amp, grad_decay], axis=0
    )
    total = lax.psum(packed, "ctx")
    grad_taps = total[: tap_count * triple].reshape(tap_count, triple, width)
    grad_amp = total[tap_count * triple : tap_count * triple + modes]
    grad_decay = total[tap_count * triple + modes :]
    grad_residues = (grad_amp * half_rate).reshape(modes, width)
    grad_log_rate = (0.5 * grad_amp * amp - grad_decay * amp * decay * rate).reshape(modes, width)
    return (
        grad_features.astype(BF16).reshape(length, triple, width),
        grad_taps,
        grad_residues,
        grad_log_rate,
        grad_weight_t,
    )


def solution(mesh):
    return jax.shard_map(
        per_device,
        mesh=mesh,
        in_specs=(
            P("ctx", None, "tp"),
            P(None, None, "tp"),
            P(None, "tp"),
            P(None, "tp"),
            P("tp", None),
            P("ctx", "tp"),
        ),
        out_specs=(
            P("ctx", None, "tp"),
            P(None, None, "tp"),
            P(None, "tp"),
            P(None, "tp"),
            P("ctx", "tp"),
        ),
        check_vma=False,
    )
```

```python
import jax
import jax.numpy as jnp
from jax import lax
from jax.experimental import pallas as pl
from jax.experimental.pallas import tpu as pltpu
from jax.sharding import PartitionSpec as P

F32 = jnp.float32
BF16 = jnp.bfloat16
LANES = 128


def shifted(value, axis, steps):
    count = lax.axis_size(axis)
    first, last = (max(0, -steps), min(count, count - steps))
    return lax.ppermute(value, axis, [(source, source + steps) for source in range(first, last)])


def rounded(value):
    return value.astype(BF16).astype(F32)


def peer(offset):
    count = lax.axis_size("ctx")
    return lax.rem(lax.axis_index("ctx") + offset + count, count)


def greet():
    barrier = pltpu.get_barrier_semaphore()
    for offset in range(1, lax.axis_size("ctx")):
        pl.semaphore_signal(
            barrier, inc=1, device_id={"ctx": peer(offset)}, device_id_type=pl.DeviceIdType.MESH
        )


def await_greetings():
    pl.semaphore_wait(pltpu.get_barrier_semaphore(), lax.axis_size("ctx") - 1)


def push(source, target, send_sem, recv_sem, offset):
    copy = pltpu.make_async_remote_copy(
        src_ref=source,
        dst_ref=target,
        send_sem=send_sem,
        recv_sem=recv_sem,
        device_id={"ctx": peer(offset)},
        device_id_type=pl.DeviceIdType.MESH,
    )
    copy.start()
    return copy


def tree_sum(terms):
    while len(terms) > 1:
        pairs = [terms[i] + terms[i + 1] for i in range(0, len(terms) - 1, 2)]
        terms = pairs + terms[len(terms) - len(terms) % 2 :]
    return terms[0]


def forward_kernel(
    padded_ref, taps_ref, decay_ref, block_decay_ref, amp_ref,
    short_ref, gated_ref, convolved_ref, past_ref,
    own, arrived, send_sems, recv_sems,
):
    modes = decay_ref.shape[0]
    length = short_ref.shape[0]
    tap_count = taps_ref.shape[0]
    count = lax.axis_size("ctx")
    position = lax.axis_index("ctx")
    greet()

    def filter_step(t, carry):
        for j in range(3):
            total = taps_ref[0, j] * padded_ref[t + tap_count - 1, j]
            for lag in range(1, tap_count):
                total = total + taps_ref[lag, j] * padded_ref[t + tap_count - 1 - lag, j]
            short_ref[t, j] = total
        return carry

    lax.fori_loop(0, length, filter_step, 0, unroll=4)
    decays = [decay_ref[r] for r in range(modes)]
    zero = jnp.zeros(decay_ref.shape[1:], F32)

    def local_step(t, states):
        product = rounded(short_ref[t, 1] * short_ref[t, 2])
        return tuple(decays[r] * states[r] + product for r in range(modes))

    final = lax.fori_loop(0, length, local_step, (zero,) * modes, unroll=4)
    for r in range(modes):
        own[r] = final[r]

    await_greetings()
    copies = [
        push(own, arrived.at[position], send_sems.at[k], recv_sems.at[k], k)
        for k in range(1, count)
    ]
    arrived[position] = own[...]
    for copy in copies:
        copy.wait()
    past_ref[...] = jnp.zeros(past_ref.shape, F32)
    for block in range(count - 1):
        past_ref[...] = jnp.where(
            block < position, block_decay_ref[...] * past_ref[...] + arrived[block], past_ref[...]
        )

    def step(t, states):
        product = rounded(short_ref[t, 1] * short_ref[t, 2])
        new = tuple(decays[r] * states[r] + product for r in range(modes))
        convolved = rounded(tree_sum([amp_ref[r] * new[r] for r in range(modes)]))
        convolved_ref[t] = convolved
        gated_ref[t] = short_ref[t, 0] * convolved
        return new

    lax.fori_loop(0, length, step, tuple(past_ref[r] for r in range(modes)), unroll=2)


def backward_kernel(
    padded_ref, short_ref, convolved_ref, grad_gated_ref, taps_ref, decay_ref, block_decay_ref,
    amp_ref, past_ref,
    grad_features_ref, total_ref,
    own, arrived, future, history, grad_conv, grad_short, readout, tail, packed, pieces, summed,
    state_send, state_recv, piece_send, piece_recv, sum_send, sum_recv, tail_send, tail_recv,
):
    modes = decay_ref.shape[0]
    length = short_ref.shape[0]
    tap_count = taps_ref.shape[0]
    share = summed.shape[0]
    count = lax.axis_size("ctx")
    position = lax.axis_index("ctx")
    zero = jnp.zeros(decay_ref.shape[1:], F32)
    decays = [decay_ref[r] for r in range(modes)]
    greet()

    def local_step(i, states):
        t = length - 1 - i
        grad = rounded(grad_gated_ref[t] * short_ref[t, 0])
        grad_conv[t] = grad
        return tuple(decays[r] * states[r] + grad for r in range(modes))

    final = lax.fori_loop(0, length, local_step, (zero,) * modes, unroll=4)
    for r in range(modes):
        own[r] = final[r]
    await_greetings()
    copies = [
        push(own, arrived.at[position], state_send.at[k], state_recv.at[k], k)
        for k in range(1, count)
    ]
    arrived[position] = own[...]

    for r in range(modes):
        history[0, r] = past_ref[r]

    def forward(t, states):
        product = rounded(short_ref[t, 1] * short_ref[t, 2])
        new = tuple(decays[r] * states[r] + product for r in range(modes))
        for r in range(modes):
            history[t + 1, r] = new[r]
        grad_short[t, 0] = grad_gated_ref[t] * convolved_ref[t]
        return new

    lax.fori_loop(0, length, forward, tuple(past_ref[r] for r in range(modes)), unroll=2)

    for copy in copies:
        copy.wait()
    future[...] = jnp.zeros(future.shape, F32)
    for block in range(count - 1, 0, -1):
        future[...] = jnp.where(
            block > position, block_decay_ref[...] * future[...] + arrived[block], future[...]
        )

    half = modes // 2
    base = 3 * tap_count
    for group in range(2):
        picks = list(range(group * half, group * half + half))

        def backward(i, carry):
            t = length - 1 - i
            states, grad_amp, grad_decay = carry
            grad = grad_conv[t]
            new = tuple(decays[r] * states[k] + grad for k, r in enumerate(picks))
            term = tree_sum([amp_ref[r] * new[k] for k, r in enumerate(picks)])
            grad_amp = tuple(grad_amp[k] + grad * history[t + 1, r] for k, r in enumerate(picks))
            grad_decay = tuple(grad_decay[k] + new[k] * history[t, r] for k, r in enumerate(picks))
            if group == 0:
                readout[t] = term
            else:
                grad_product = rounded(readout[t] + term)
                grad_short[t, 1] = grad_product * short_ref[t, 2]
                grad_short[t, 2] = grad_product * short_ref[t, 1]
            return new, grad_amp, grad_decay

        start = (tuple(future[r] for r in picks), (zero,) * half, (zero,) * half)
        unused, grad_amp, grad_decay = lax.fori_loop(0, length, backward, start, unroll=2)
        for k, r in enumerate(picks):
            packed[base + r] = grad_amp[k]
            packed[base + modes + r] = grad_decay[k]

    tail_copy = push(
        grad_short.at[pl.ds(0, tap_count - 1)], tail, tail_send.at[0], tail_recv.at[0], -1
    )

    def taps_step(t, sums):
        new = []
        for j in range(3):
            grad = grad_short[t, j]
            for lag in range(tap_count):
                new.append(sums[j * tap_count + lag] + grad * padded_ref[t + tap_count - 1 - lag, j])
        return tuple(new)

    sums = lax.fori_loop(0, length, taps_step, (zero,) * base, unroll=4)
    for j in range(3):
        for lag in range(tap_count):
            packed[lag * 3 + j] = sums[j * tap_count + lag]
    for extra in range(base + 2 * modes, packed.shape[0]):
        packed[extra] = zero

    copies = [
        push(
            packed.at[pl.ds(peer(k) * share, share)], pieces.at[position],
            piece_send.at[k], piece_recv.at[k], k,
        )
        for k in range(1, count)
    ]
    pieces[position] = packed[pl.ds(position * share, share)]

    def features_step(t, carry):
        for j in range(3):
            total = taps_ref[0, j] * grad_short[t, j]
            for lag in range(1, tap_count):
                total = total + taps_ref[lag, j] * grad_short[t + lag, j]
            grad_features_ref[t, j] = total
        return carry

    lax.fori_loop(0, length - tap_count + 1, features_step, 0, unroll=2)

    for copy in copies:
        copy.wait()
    summed[...] = tree_sum([pieces[block] for block in range(count)])
    copies = [
        push(
            summed, total_ref.at[pl.ds(position * share, share)],
            sum_send.at[k], sum_recv.at[k], k,
        )
        for k in range(1, count)
    ]
    total_ref[pl.ds(position * share, share)] = summed[...]

    tail_copy.wait()
    inner = position < count - 1
    for t in range(length - tap_count + 1, length):
        for j in range(3):
            total = taps_ref[0, j] * grad_short[t, j]
            for lag in range(1, tap_count):
                if t + lag < length:
                    later = grad_short[t + lag, j]
                else:
                    later = jnp.where(inner, tail[t + lag - length, j], 0.0)
                total = total + taps_ref[lag, j] * later
            grad_features_ref[t, j] = total
    for copy in copies:
        copy.wait()


def call(kernel, outs, scratch, identity, mib=48):
    return pl.pallas_call(
        kernel,
        out_shape=[jax.ShapeDtypeStruct(shape, F32) for shape in outs],
        scratch_shapes=[
            pltpu.SemaphoreType.DMA((item,)) if isinstance(item, int) else pltpu.VMEM(item, F32)
            for item in scratch
        ],
        compiler_params=pltpu.CompilerParams(
            vmem_limit_bytes=mib * 2**20, collective_id=identity, has_side_effects=True
        ),
    )


def per_device(features, short_taps, residues, log_rate, out_weight, grad_out):
    length, triple, width = features.shape
    tap_count = short_taps.shape[0]
    modes = residues.shape[0]
    groups = lax.axis_size("ctx")
    ranks = lax.axis_size("tp")
    rank = lax.axis_index("tp")
    rows = width // LANES
    tile = (rows, LANES)
    state = (modes,) + tile

    cotangent = lax.all_gather(grad_out, "tp", axis=1, tiled=True)
    rim_rows = shifted(features[length - (tap_count - 1) :], "ctx", 1)
    padded = jnp.concatenate([rim_rows, features], axis=0).astype(F32)
    padded = padded.reshape((length + tap_count - 1, triple) + tile)
    taps = short_taps.reshape((tap_count, triple) + tile)
    half_rate = jnp.exp(0.5 * log_rate).reshape(state)
    rate = jnp.exp(log_rate).reshape(state)
    amp = residues.reshape(state) * half_rate
    decay = jnp.exp(-rate)
    block_decay = jnp.exp(-rate * length)

    short, gated, convolved, past = call(
        forward_kernel,
        [(length, triple) + tile, (length,) + tile, (length,) + tile, state],
        [state, (groups,) + state, groups, groups],
        0,
    )(padded, taps, decay, block_decay, amp)
    gated_all = lax.all_gather(
        gated.astype(BF16).reshape(length, width), "ctx", axis=0, tiled=True
    )

    grad_gated = lax.dot_general(
        cotangent, out_weight, (((1,), (1,)), ((), ())), preferred_element_type=F32
    ).reshape((length,) + tile)

    features_out = cotangent.shape[1]
    portion = features_out // (groups * ranks)
    mine = lax.dynamic_index_in_dim(
        cotangent.reshape(length, groups, ranks, portion), rank, 2, keepdims=False
    )
    swapped = lax.all_to_all(
        mine.reshape(length, groups * portion), "ctx", split_axis=1, concat_axis=0, tiled=True
    )
    block_cotangent = lax.all_gather(swapped, "tp", axis=1, tiled=True)

    base = tap_count * triple
    share = -(-(base + 2 * modes) // groups)
    grad_features, total = call(
        backward_kernel,
        [(length, triple) + tile, (groups * share,) + tile],
        [
            state, (groups,) + state, state, (length + 1,) + state, (length,) + tile,
            (length, triple) + tile, (length,) + tile, (tap_count - 1, triple) + tile,
            (groups * share,) + tile, (groups, share) + tile, (share,) + tile,
            groups, groups, groups, groups, groups, groups, 1, 1,
        ],
        1,
    )(padded, short, convolved, grad_gated, taps, decay, block_decay, amp, past)

    grad_weight_t = lax.dot_general(
        block_cotangent, gated_all, (((0,), (0,)), ((), ())), preferred_element_type=F32
    )
    grad_taps = total[:base].reshape(tap_count, triple, width)
    grad_amp = total[base : base + modes]
    grad_decay = total[base + modes : base + 2 * modes]
    grad_residues = (grad_amp * half_rate).reshape(modes, width)
    grad_log_rate = (0.5 * grad_amp * amp - grad_decay * amp * decay * rate).reshape(modes, width)
    return (
        grad_features.astype(BF16).reshape(length, triple, width),
        grad_taps,
        grad_residues,
        grad_log_rate,
        grad_weight_t,
    )


def solution(mesh):
    return jax.shard_map(
        per_device,
        mesh=mesh,
        in_specs=(
            P("ctx", None, "tp"),
            P(None, None, "tp"),
            P(None, "tp"),
            P(None, "tp"),
            P("tp", None),
            P("ctx", "tp"),
        ),
        out_specs=(
            P("ctx", None, "tp"),
            P(None, None, "tp"),
            P(None, "tp"),
            P(None, "tp"),
            P("ctx", "tp"),
        ),
        check_vma=False,
    )
```

```python
import jax
import jax.numpy as jnp
from jax import lax
from jax.experimental import pallas as pl
from jax.experimental.pallas import tpu as pltpu
from jax.sharding import PartitionSpec as P

F32 = jnp.float32
BF16 = jnp.bfloat16
LANES = 128


def rounded(value):
    return value.astype(BF16).astype(F32)


def peer(offset, axis="ctx"):
    count = lax.axis_size(axis)
    return lax.rem(lax.axis_index(axis) + offset + count, count)


def greet(axes):
    barrier = pltpu.get_barrier_semaphore()
    for axis in axes:
        for offset in range(1, lax.axis_size(axis)):
            pl.semaphore_signal(
                barrier,
                inc=1,
                device_id={axis: peer(offset, axis)},
                device_id_type=pl.DeviceIdType.MESH,
            )


def await_greetings(axes):
    pl.semaphore_wait(
        pltpu.get_barrier_semaphore(), sum(lax.axis_size(axis) - 1 for axis in axes)
    )


def remote(source, target, send_sem, recv_sem, offset, axis="ctx"):
    return pltpu.make_async_remote_copy(
        src_ref=source,
        dst_ref=target,
        send_sem=send_sem,
        recv_sem=recv_sem,
        device_id={axis: peer(offset, axis)},
        device_id_type=pl.DeviceIdType.MESH,
    )


def push(*arguments):
    copy = remote(*arguments)
    copy.start()
    return copy


def send_states(own, arrived, send_sems, recv_sems, direction):
    count = lax.axis_size("ctx")
    position = lax.axis_index("ctx")
    sends = []
    for k in range(1, count):
        copy = remote(own, arrived.at[position], send_sems.at[k], recv_sems.at[k], direction * k)
        if direction > 0:
            has_target, has_source = position + k < count, position >= k
        else:
            has_target, has_source = position >= k, position + k < count

        @pl.when(has_target)
        def start():
            copy.start()

        sends.append((copy, has_target, has_source))
    return sends


def await_states(sends):
    for copy, has_target, has_source in sends:

        @pl.when(has_source)
        def received():
            copy.wait_recv()

        @pl.when(has_target)
        def sent():
            copy.wait_send()


def carry_states(state, arrived, block_decay, direction):
    count = lax.axis_size("ctx")
    position = lax.axis_index("ctx")
    state[...] = jnp.zeros(state.shape, F32)
    for block in range(count - 1) if direction > 0 else range(count - 1, 0, -1):

        @pl.when(block < position if direction > 0 else block > position)
        def add():
            state[...] = block_decay[...] * state[...] + arrived[block]


def tree_sum(terms):
    while len(terms) > 1:
        pairs = [terms[i] + terms[i + 1] for i in range(0, len(terms) - 1, 2)]
        terms = pairs + terms[len(terms) - len(terms) % 2 :]
    return terms[0]


def forward_kernel(
    features_ref, taps_ref, decay_ref, block_decay_ref, amp_ref,
    short_ref, gated_ref, convolved_ref, past_ref, padded_ref,
    own, arrived, send_sems, recv_sems, rim_send, rim_recv,
):
    modes = decay_ref.shape[0]
    length = short_ref.shape[0]
    tap_count = taps_ref.shape[0]
    rim = tap_count - 1
    greet(("ctx",))

    def copy_step(t, carry):
        for j in range(3):
            padded_ref[t + rim, j] = features_ref[t, j]
        return carry

    lax.fori_loop(0, length, copy_step, 0, unroll=4)
    await_greetings(("ctx",))
    rim_copy = push(
        features_ref.at[pl.ds(length - rim, rim)], padded_ref.at[pl.ds(0, rim)],
        rim_send.at[0], rim_recv.at[0], 1,
    )

    def filter_step(t, carry):
        for j in range(3):
            total = taps_ref[0, j] * padded_ref[t + rim, j]
            for lag in range(1, tap_count):
                total = total + taps_ref[lag, j] * padded_ref[t + rim - lag, j]
            short_ref[t, j] = total
        return carry

    lax.fori_loop(rim, length, filter_step, 0, unroll=2)
    rim_copy.wait()

    @pl.when(lax.axis_index("ctx") == 0)
    def clear():
        padded_ref[pl.ds(0, rim)] = jnp.zeros((rim,) + padded_ref.shape[1:], F32)

    for t in range(rim):
        filter_step(t, 0)
    decays = [decay_ref[r] for r in range(modes)]
    zero = jnp.zeros(decay_ref.shape[1:], F32)

    def local_step(t, states):
        product = rounded(short_ref[t, 1] * short_ref[t, 2])
        return tuple(decays[r] * states[r] + product for r in range(modes))

    final = lax.fori_loop(0, length, local_step, (zero,) * modes, unroll=4)
    for r in range(modes):
        own[r] = final[r]

    await_states(send_states(own, arrived, send_sems, recv_sems, 1))
    carry_states(past_ref, arrived, block_decay_ref, 1)

    def step(t, states):
        product = rounded(short_ref[t, 1] * short_ref[t, 2])
        new = tuple(decays[r] * states[r] + product for r in range(modes))
        convolved = rounded(tree_sum([amp_ref[r] * new[r] for r in range(modes)]))
        convolved_ref[t] = convolved
        gated_ref[t] = short_ref[t, 0] * convolved
        return new

    lax.fori_loop(0, length, step, tuple(past_ref[r] for r in range(modes)), unroll=2)


def backward_kernel(
    padded_ref, short_ref, convolved_ref, grad_gated_ref, taps_ref, decay_ref, block_decay_ref,
    amp_ref, past_ref, mine_ref,
    grad_features_ref, total_ref, block_ref,
    own, arrived, future, history, grad_conv, grad_short, readout, tail, packed, pieces, summed,
    state_send, state_recv, piece_send, piece_recv, sum_send, sum_recv, tail_send, tail_recv,
    swap_send, swap_recv, spread_send, spread_recv,
):
    modes = decay_ref.shape[0]
    length = short_ref.shape[0]
    tap_count = taps_ref.shape[0]
    share = summed.shape[0]
    count = lax.axis_size("ctx")
    position = lax.axis_index("ctx")
    zero = jnp.zeros(decay_ref.shape[1:], F32)
    decays = [decay_ref[r] for r in range(modes)]
    ranks = lax.axis_size("tp")
    rank = lax.axis_index("tp")
    greet(("ctx", "tp"))

    def local_step(i, states):
        t = length - 1 - i
        grad = rounded(grad_gated_ref[t] * short_ref[t, 0])
        grad_conv[t] = grad
        return tuple(decays[r] * states[r] + grad for r in range(modes))

    final = lax.fori_loop(0, length, local_step, (zero,) * modes, unroll=4)
    for r in range(modes):
        own[r] = final[r]
    await_greetings(("ctx", "tp"))
    sends = send_states(own, arrived, state_send, state_recv, -1)
    swaps = [
        push(
            mine_ref.at[peer(k)], block_ref.at[rank, position], swap_send.at[k], swap_recv.at[k], k
        )
        for k in range(1, count)
    ]
    block_ref[rank, position] = mine_ref[position]

    for r in range(modes):
        history[0, r] = past_ref[r]

    def forward(t, states):
        product = rounded(short_ref[t, 1] * short_ref[t, 2])
        new = tuple(decays[r] * states[r] + product for r in range(modes))
        for r in range(modes):
            history[t + 1, r] = new[r]
        grad_short[t, 0] = grad_gated_ref[t] * convolved_ref[t]
        return new

    lax.fori_loop(0, length, forward, tuple(past_ref[r] for r in range(modes)), unroll=2)

    await_states(sends)
    carry_states(future, arrived, block_decay_ref, -1)

    half = modes // 2
    base = 3 * tap_count
    for group in range(2):
        picks = list(range(group * half, group * half + half))

        def backward(i, carry):
            t = length - 1 - i
            states, grad_amp, grad_decay = carry
            grad = grad_conv[t]
            new = tuple(decays[r] * states[k] + grad for k, r in enumerate(picks))
            term = tree_sum([amp_ref[r] * new[k] for k, r in enumerate(picks)])
            grad_amp = tuple(grad_amp[k] + grad * history[t + 1, r] for k, r in enumerate(picks))
            grad_decay = tuple(grad_decay[k] + new[k] * history[t, r] for k, r in enumerate(picks))
            if group == 0:
                readout[t] = term
            else:
                grad_product = rounded(readout[t] + term)
                grad_short[t, 1] = grad_product * short_ref[t, 2]
                grad_short[t, 2] = grad_product * short_ref[t, 1]
            return new, grad_amp, grad_decay

        if group == 1:
            for copy in swaps:
                copy.wait()
            spreads = [
                push(
                    block_ref.at[rank], block_ref.at[rank],
                    spread_send.at[k], spread_recv.at[k], k, "tp",
                )
                for k in range(1, ranks)
            ]

        start = (tuple(future[r] for r in picks), (zero,) * half, (zero,) * half)
        unused, grad_amp, grad_decay = lax.fori_loop(0, length, backward, start, unroll=2)
        for k, r in enumerate(picks):
            packed[base + r] = grad_amp[k]
            packed[base + modes + r] = grad_decay[k]

    tail_copy = push(
        grad_short.at[pl.ds(0, tap_count - 1)], tail, tail_send.at[0], tail_recv.at[0], -1
    )

    def taps_step(t, sums):
        new = []
        for j in range(3):
            grad = grad_short[t, j]
            for lag in range(tap_count):
                new.append(sums[j * tap_count + lag] + grad * padded_ref[t + tap_count - 1 - lag, j])
        return tuple(new)

    sums = lax.fori_loop(0, length, taps_step, (zero,) * base, unroll=4)
    for j in range(3):
        for lag in range(tap_count):
            packed[lag * 3 + j] = sums[j * tap_count + lag]
    for extra in range(base + 2 * modes, packed.shape[0]):
        packed[extra] = zero

    copies = [
        push(
            packed.at[pl.ds(peer(k) * share, share)], pieces.at[position],
            piece_send.at[k], piece_recv.at[k], k,
        )
        for k in range(1, count)
    ]
    pieces[position] = packed[pl.ds(position * share, share)]

    def features_step(t, carry):
        for j in range(3):
            total = taps_ref[0, j] * grad_short[t, j]
            for lag in range(1, tap_count):
                total = total + taps_ref[lag, j] * grad_short[t + lag, j]
            grad_features_ref[t, j] = total
        return carry

    lax.fori_loop(0, length - tap_count + 1, features_step, 0, unroll=2)

    for copy in copies:
        copy.wait()
    summed[...] = tree_sum([pieces[block] for block in range(count)])
    copies = [
        push(
            summed, total_ref.at[pl.ds(position * share, share)],
            sum_send.at[k], sum_recv.at[k], k,
        )
        for k in range(1, count)
    ]
    total_ref[pl.ds(position * share, share)] = summed[...]

    tail_copy.wait()
    inner = position < count - 1
    for t in range(length - tap_count + 1, length):
        for j in range(3):
            total = taps_ref[0, j] * grad_short[t, j]
            for lag in range(1, tap_count):
                if t + lag < length:
                    later = grad_short[t + lag, j]
                else:
                    later = jnp.where(inner, tail[t + lag - length, j], 0.0)
                total = total + taps_ref[lag, j] * later
            grad_features_ref[t, j] = total
    for copy in copies + spreads:
        copy.wait()


def call(kernel, outs, scratch, identity, mib=48):
    return pl.pallas_call(
        kernel,
        out_shape=[
            item if isinstance(item, jax.ShapeDtypeStruct) else jax.ShapeDtypeStruct(item, F32)
            for item in outs
        ],
        scratch_shapes=[
            pltpu.SemaphoreType.DMA((item,)) if isinstance(item, int) else pltpu.VMEM(item, F32)
            for item in scratch
        ],
        compiler_params=pltpu.CompilerParams(
            vmem_limit_bytes=mib * 2**20, collective_id=identity, has_side_effects=True
        ),
    )


def per_device(features, short_taps, residues, log_rate, out_weight, grad_out):
    length, triple, width = features.shape
    tap_count = short_taps.shape[0]
    modes = residues.shape[0]
    groups = lax.axis_size("ctx")
    ranks = lax.axis_size("tp")
    rank = lax.axis_index("tp")
    rows = width // LANES
    tile = (rows, LANES)
    state = (modes,) + tile

    cotangent = lax.all_gather(grad_out, "tp", axis=1, tiled=True)
    values = features.astype(F32).reshape((length, triple) + tile)
    taps = short_taps.reshape((tap_count, triple) + tile)
    half_rate = jnp.exp(0.5 * log_rate).reshape(state)
    rate = jnp.exp(log_rate).reshape(state)
    amp = residues.reshape(state) * half_rate
    decay = jnp.exp(-rate)
    block_decay = jnp.exp(-rate * length)

    short, gated, convolved, past, padded = call(
        forward_kernel,
        [
            (length, triple) + tile, (length,) + tile, (length,) + tile, state,
            (length + tap_count - 1, triple) + tile,
        ],
        [state, (groups,) + state, groups, groups, 1, 1],
        0,
    )(values, taps, decay, block_decay, amp)
    gated_all = lax.all_gather(
        gated.astype(BF16).reshape(length, width), "ctx", axis=0, tiled=True
    )

    grad_gated = lax.dot_general(
        cotangent, out_weight, (((1,), (1,)), ((), ())), preferred_element_type=F32
    ).reshape((length,) + tile)

    features_out = cotangent.shape[1]
    portion = features_out // (groups * ranks)
    mine = jnp.stack(
        [
            lax.dynamic_slice_in_dim(cotangent, (group * ranks + rank) * portion, portion, 1)
            for group in range(groups)
        ]
    )

    base = tap_count * triple
    share = -(-(base + 2 * modes) // groups)
    grad_features, total, block_cotangent = call(
        backward_kernel,
        [
            (length, triple) + tile,
            (groups * share,) + tile,
            jax.ShapeDtypeStruct((ranks, groups, length, portion), BF16),
        ],
        [
            state, (groups,) + state, state, (length + 1,) + state, (length,) + tile,
            (length, triple) + tile, (length,) + tile, (tap_count - 1, triple) + tile,
            (groups * share,) + tile, (groups, share) + tile, (share,) + tile,
            groups, groups, groups, groups, groups, groups, 1, 1, groups, groups, ranks, ranks,
        ],
        1,
    )(padded, short, convolved, grad_gated, taps, decay, block_decay, amp, past, mine)

    grad_weight_t = lax.dot_general(
        block_cotangent.reshape(ranks, groups * length, portion),
        gated_all,
        (((1,), (0,)), ((), ())),
        preferred_element_type=F32,
    ).reshape(ranks * portion, width)
    grad_taps = total[:base].reshape(tap_count, triple, width)
    grad_amp = total[base : base + modes]
    grad_decay = total[base + modes : base + 2 * modes]
    grad_residues = (grad_amp * half_rate).reshape(modes, width)
    grad_log_rate = (0.5 * grad_amp * amp - grad_decay * amp * decay * rate).reshape(modes, width)
    return (
        grad_features.astype(BF16).reshape(length, triple, width),
        grad_taps,
        grad_residues,
        grad_log_rate,
        grad_weight_t,
    )


def solution(mesh):
    return jax.shard_map(
        per_device,
        mesh=mesh,
        in_specs=(
            P("ctx", None, "tp"),
            P(None, None, "tp"),
            P(None, "tp"),
            P(None, "tp"),
            P("tp", None),
            P("ctx", "tp"),
        ),
        out_specs=(
            P("ctx", None, "tp"),
            P(None, None, "tp"),
            P(None, "tp"),
            P(None, "tp"),
            P("ctx", "tp"),
        ),
        check_vma=False,
    )
```

```python
import jax
import jax.numpy as jnp
from jax import lax
from jax.experimental import pallas as pl
from jax.experimental.pallas import tpu as pltpu
from jax.sharding import PartitionSpec as P

F32 = jnp.float32
BF16 = jnp.bfloat16
LANES = 128


def rounded(value):
    return value.astype(BF16).astype(F32)


def peer(offset, axis="ctx"):
    count = lax.axis_size(axis)
    return lax.rem(lax.axis_index(axis) + offset + count, count)


def greet(axes):
    barrier = pltpu.get_barrier_semaphore()
    for axis in axes:
        for offset in range(1, lax.axis_size(axis)):
            pl.semaphore_signal(
                barrier,
                inc=1,
                device_id={axis: peer(offset, axis)},
                device_id_type=pl.DeviceIdType.MESH,
            )


def await_greetings(axes):
    pl.semaphore_wait(
        pltpu.get_barrier_semaphore(), sum(lax.axis_size(axis) - 1 for axis in axes)
    )


def remote(source, target, send_sem, recv_sem, offset, axis="ctx"):
    return pltpu.make_async_remote_copy(
        src_ref=source,
        dst_ref=target,
        send_sem=send_sem,
        recv_sem=recv_sem,
        device_id={axis: peer(offset, axis)},
        device_id_type=pl.DeviceIdType.MESH,
    )


def push(*arguments):
    copy = remote(*arguments)
    copy.start()
    return copy


def send_states(own, arrived, send_sems, recv_sems, direction):
    count = lax.axis_size("ctx")
    position = lax.axis_index("ctx")
    sends = []
    for k in range(1, count):
        copy = remote(own, arrived.at[position], send_sems.at[k], recv_sems.at[k], direction * k)
        if direction > 0:
            has_target, has_source = position + k < count, position >= k
        else:
            has_target, has_source = position >= k, position + k < count

        @pl.when(has_target)
        def start():
            copy.start()

        sends.append((copy, has_target, has_source))
    return sends


def await_states(sends):
    for copy, has_target, has_source in sends:

        @pl.when(has_source)
        def received():
            copy.wait_recv()

        @pl.when(has_target)
        def sent():
            copy.wait_send()


def carry_states(state, arrived, block_decay, direction):
    count = lax.axis_size("ctx")
    position = lax.axis_index("ctx")
    state[...] = jnp.zeros(state.shape, F32)
    for block in range(count - 1) if direction > 0 else range(count - 1, 0, -1):

        @pl.when(block < position if direction > 0 else block > position)
        def add():
            state[...] = block_decay[...] * state[...] + arrived[block]


def tree_sum(terms):
    while len(terms) > 1:
        pairs = [terms[i] + terms[i + 1] for i in range(0, len(terms) - 1, 2)]
        terms = pairs + terms[len(terms) - len(terms) % 2 :]
    return terms[0]


def forward_kernel(
    features_ref, taps_ref, decay_ref, block_decay_ref, amp_ref,
    short_ref, gated_ref, convolved_ref, past_ref, padded_ref,
    own, arrived, send_sems, recv_sems, rim_send, rim_recv,
):
    modes = decay_ref.shape[0]
    length = short_ref.shape[0]
    tap_count = taps_ref.shape[0]
    rim = tap_count - 1
    greet(("ctx",))

    def copy_step(t, carry):
        for j in range(3):
            padded_ref[t + rim, j] = features_ref[t, j]
        return carry

    lax.fori_loop(0, length, copy_step, 0, unroll=4)
    await_greetings(("ctx",))
    rim_copy = push(
        features_ref.at[pl.ds(length - rim, rim)], padded_ref.at[pl.ds(0, rim)],
        rim_send.at[0], rim_recv.at[0], 1,
    )

    def filter_step(t, carry):
        for j in range(3):
            total = taps_ref[0, j] * padded_ref[t + rim, j]
            for lag in range(1, tap_count):
                total = total + taps_ref[lag, j] * padded_ref[t + rim - lag, j]
            short_ref[t, j] = total
        return carry

    lax.fori_loop(rim, length, filter_step, 0, unroll=2)
    rim_copy.wait()

    @pl.when(lax.axis_index("ctx") == 0)
    def clear():
        padded_ref[pl.ds(0, rim)] = jnp.zeros((rim,) + padded_ref.shape[1:], F32)

    for t in range(rim):
        filter_step(t, 0)
    decays = [decay_ref[r] for r in range(modes)]
    zero = jnp.zeros(decay_ref.shape[1:], F32)

    def local_step(t, states):
        product = rounded(short_ref[t, 1] * short_ref[t, 2])
        return tuple(decays[r] * states[r] + product for r in range(modes))

    final = lax.fori_loop(0, length, local_step, (zero,) * modes, unroll=4)
    for r in range(modes):
        own[r] = final[r]

    await_states(send_states(own, arrived, send_sems, recv_sems, 1))
    carry_states(past_ref, arrived, block_decay_ref, 1)

    def step(t, states):
        product = rounded(short_ref[t, 1] * short_ref[t, 2])
        new = tuple(decays[r] * states[r] + product for r in range(modes))
        convolved = rounded(tree_sum([amp_ref[r] * new[r] for r in range(modes)]))
        convolved_ref[t] = convolved
        gated_ref[t] = short_ref[t, 0] * convolved
        return new

    lax.fori_loop(0, length, step, tuple(past_ref[r] for r in range(modes)), unroll=2)


def backward_kernel(
    padded_ref, short_ref, convolved_ref, grad_gated_ref, taps_ref, decay_ref, block_decay_ref,
    amp_ref, past_ref,
    grad_features_ref, total_ref,
    own, arrived, future, history, grad_conv, grad_short, readout, tail, packed, pieces, summed,
    state_send, state_recv, piece_send, piece_recv, sum_send, sum_recv, tail_send, tail_recv,
):
    modes = decay_ref.shape[0]
    length = short_ref.shape[0]
    tap_count = taps_ref.shape[0]
    share = summed.shape[0]
    count = lax.axis_size("ctx")
    position = lax.axis_index("ctx")
    zero = jnp.zeros(decay_ref.shape[1:], F32)
    decays = [decay_ref[r] for r in range(modes)]
    greet(("ctx",))

    def local_step(i, states):
        t = length - 1 - i
        grad = rounded(grad_gated_ref[t] * short_ref[t, 0])
        grad_conv[t] = grad
        return tuple(decays[r] * states[r] + grad for r in range(modes))

    final = lax.fori_loop(0, length, local_step, (zero,) * modes, unroll=4)
    for r in range(modes):
        own[r] = final[r]
    await_greetings(("ctx",))
    sends = send_states(own, arrived, state_send, state_recv, -1)
    for r in range(modes):
        history[0, r] = past_ref[r]

    def forward(t, states):
        product = rounded(short_ref[t, 1] * short_ref[t, 2])
        new = tuple(decays[r] * states[r] + product for r in range(modes))
        for r in range(modes):
            history[t + 1, r] = new[r]
        grad_short[t, 0] = grad_gated_ref[t] * convolved_ref[t]
        return new

    lax.fori_loop(0, length, forward, tuple(past_ref[r] for r in range(modes)), unroll=2)

    await_states(sends)
    carry_states(future, arrived, block_decay_ref, -1)

    half = modes // 2
    base = 3 * tap_count
    for group in range(2):
        picks = list(range(group * half, group * half + half))

        def backward(i, carry):
            t = length - 1 - i
            states, grad_amp, grad_decay = carry
            grad = grad_conv[t]
            new = tuple(decays[r] * states[k] + grad for k, r in enumerate(picks))
            term = tree_sum([amp_ref[r] * new[k] for k, r in enumerate(picks)])
            grad_amp = tuple(grad_amp[k] + grad * history[t + 1, r] for k, r in enumerate(picks))
            grad_decay = tuple(grad_decay[k] + new[k] * history[t, r] for k, r in enumerate(picks))
            if group == 0:
                readout[t] = term
            else:
                grad_product = rounded(readout[t] + term)
                grad_short[t, 1] = grad_product * short_ref[t, 2]
                grad_short[t, 2] = grad_product * short_ref[t, 1]
            return new, grad_amp, grad_decay

        start = (tuple(future[r] for r in picks), (zero,) * half, (zero,) * half)
        unused, grad_amp, grad_decay = lax.fori_loop(0, length, backward, start, unroll=2)
        for k, r in enumerate(picks):
            packed[base + r] = grad_amp[k]
            packed[base + modes + r] = grad_decay[k]

    tail_copy = push(
        grad_short.at[pl.ds(0, tap_count - 1)], tail, tail_send.at[0], tail_recv.at[0], -1
    )

    def taps_step(t, sums):
        new = []
        for j in range(3):
            grad = grad_short[t, j]
            for lag in range(tap_count):
                new.append(sums[j * tap_count + lag] + grad * padded_ref[t + tap_count - 1 - lag, j])
        return tuple(new)

    sums = lax.fori_loop(0, length, taps_step, (zero,) * base, unroll=4)
    for j in range(3):
        for lag in range(tap_count):
            packed[lag * 3 + j] = sums[j * tap_count + lag]
    for extra in range(base + 2 * modes, packed.shape[0]):
        packed[extra] = zero

    copies = [
        push(
            packed.at[pl.ds(peer(k) * share, share)], pieces.at[position],
            piece_send.at[k], piece_recv.at[k], k,
        )
        for k in range(1, count)
    ]
    pieces[position] = packed[pl.ds(position * share, share)]

    def features_step(t, carry):
        for j in range(3):
            total = taps_ref[0, j] * grad_short[t, j]
            for lag in range(1, tap_count):
                total = total + taps_ref[lag, j] * grad_short[t + lag, j]
            grad_features_ref[t, j] = total
        return carry

    lax.fori_loop(0, length - tap_count + 1, features_step, 0, unroll=2)

    for copy in copies:
        copy.wait()
    summed[...] = tree_sum([pieces[block] for block in range(count)])
    copies = [
        push(
            summed, total_ref.at[pl.ds(position * share, share)],
            sum_send.at[k], sum_recv.at[k], k,
        )
        for k in range(1, count)
    ]
    total_ref[pl.ds(position * share, share)] = summed[...]

    tail_copy.wait()
    inner = position < count - 1
    for t in range(length - tap_count + 1, length):
        for j in range(3):
            total = taps_ref[0, j] * grad_short[t, j]
            for lag in range(1, tap_count):
                if t + lag < length:
                    later = grad_short[t + lag, j]
                else:
                    later = jnp.where(inner, tail[t + lag - length, j], 0.0)
                total = total + taps_ref[lag, j] * later
            grad_features_ref[t, j] = total
    for copy in copies:
        copy.wait()


def call(kernel, outs, scratch, identity, mib=48):
    return pl.pallas_call(
        kernel,
        out_shape=[
            item if isinstance(item, jax.ShapeDtypeStruct) else jax.ShapeDtypeStruct(item, F32)
            for item in outs
        ],
        scratch_shapes=[
            pltpu.SemaphoreType.DMA((item,)) if isinstance(item, int) else pltpu.VMEM(item, F32)
            for item in scratch
        ],
        compiler_params=pltpu.CompilerParams(
            vmem_limit_bytes=mib * 2**20, collective_id=identity, has_side_effects=True
        ),
    )


def per_device(features, short_taps, residues, log_rate, out_weight, grad_out):
    length, triple, width = features.shape
    tap_count = short_taps.shape[0]
    modes = residues.shape[0]
    groups = lax.axis_size("ctx")
    ranks = lax.axis_size("tp")
    rank = lax.axis_index("tp")
    rows = width // LANES
    tile = (rows, LANES)
    state = (modes,) + tile

    cotangent = lax.all_gather(grad_out, "tp", axis=1, tiled=True)
    values = features.astype(F32).reshape((length, triple) + tile)
    taps = short_taps.reshape((tap_count, triple) + tile)
    half_rate = jnp.exp(0.5 * log_rate).reshape(state)
    rate = jnp.exp(log_rate).reshape(state)
    amp = residues.reshape(state) * half_rate
    decay = jnp.exp(-rate)
    block_decay = jnp.exp(-rate * length)

    short, gated, convolved, past, padded = call(
        forward_kernel,
        [
            (length, triple) + tile, (length,) + tile, (length,) + tile, state,
            (length + tap_count - 1, triple) + tile,
        ],
        [state, (groups,) + state, groups, groups, 1, 1],
        0,
    )(values, taps, decay, block_decay, amp)
    gated_all = lax.all_gather(
        gated.astype(BF16).reshape(length, width), "ctx", axis=0, tiled=True
    )

    grad_gated = lax.dot_general(
        cotangent, out_weight, (((1,), (1,)), ((), ())), preferred_element_type=F32
    ).reshape((length,) + tile)

    features_out = cotangent.shape[1]
    portion = features_out // (groups * ranks)
    mine = lax.dynamic_index_in_dim(
        cotangent.reshape(length, groups, ranks, portion), rank, 2, keepdims=False
    )
    swapped = lax.all_to_all(
        mine.reshape(length, groups * portion), "ctx", split_axis=1, concat_axis=0, tiled=True
    )
    block_cotangent = lax.all_gather(swapped, "tp", axis=1, tiled=True)

    base = tap_count * triple
    share = -(-(base + 2 * modes) // groups)
    grad_features, total = call(
        backward_kernel,
        [
            (length, triple) + tile,
            (groups * share,) + tile,
        ],
        [
            state, (groups,) + state, state, (length + 1,) + state, (length,) + tile,
            (length, triple) + tile, (length,) + tile, (tap_count - 1, triple) + tile,
            (groups * share,) + tile, (groups, share) + tile, (share,) + tile,
            groups, groups, groups, groups, groups, groups, 1, 1,
        ],
        1,
    )(padded, short, convolved, grad_gated, taps, decay, block_decay, amp, past)

    grad_weight_t = lax.dot_general(
        block_cotangent, gated_all, (((0,), (0,)), ((), ())), preferred_element_type=F32
    )
    grad_taps = total[:base].reshape(tap_count, triple, width)
    grad_amp = total[base : base + modes]
    grad_decay = total[base + modes : base + 2 * modes]
    grad_residues = (grad_amp * half_rate).reshape(modes, width)
    grad_log_rate = (0.5 * grad_amp * amp - grad_decay * amp * decay * rate).reshape(modes, width)
    return (
        grad_features.astype(BF16).reshape(length, triple, width),
        grad_taps,
        grad_residues,
        grad_log_rate,
        grad_weight_t,
    )


def solution(mesh):
    return jax.shard_map(
        per_device,
        mesh=mesh,
        in_specs=(
            P("ctx", None, "tp"),
            P(None, None, "tp"),
            P(None, "tp"),
            P(None, "tp"),
            P("tp", None),
            P("ctx", "tp"),
        ),
        out_specs=(
            P("ctx", None, "tp"),
            P(None, None, "tp"),
            P(None, "tp"),
            P(None, "tp"),
            P("ctx", "tp"),
        ),
        check_vma=False,
    )
```
